32 devices in a mesh: replica: 16 (over z, x, core), fsdp: 2 (over y).
Axes of the slice: x: 2, y: 2, z: 4, core: 2. Of those that a mesh axis runs over, the one named last changes fastest.
Arguments:
- features: bfloat16 [16, 384, 2048], P('replica', 'fsdp'), may hold values from -6 to 6
- cotangent: bfloat16 [16, 384, 2048], P('replica', 'fsdp'), may hold values from -6 to 6
- master: float32 [16, 2048, 2048], P('replica', None, 'fsdp'), may hold values from -0.75 to 0.75
- moment: bfloat16 [16, 2048, 2048], P('replica', None, 'fsdp'), may hold values from -6 to 6
- variance: float32 [16, 2048, 2048], P('replica', None, 'fsdp'), may hold values from 0.05 to 1
- step_count: int32 [1], replicated, may hold values from 1 to 24
Outputs:
- mixed: float32 [16, 2048, 2048], P('replica', None, 'fsdp')
The draws below stay inside these ranges and needn't reach their ends.
All inputs are finite; a program needn't handle non-finite values.
Results may differ from the reference program's by a relative error of at most 0.0022.
Values may be sent and summed in bfloat16 or wider, within the bound.
A program may use at most 128 MiB of HBM per device.

```python
import math
import jax
import jax.numpy as jnp
from jax import lax

D_IN = 2048
HEADS = 16
HEAD = 128
E = 2048
TOKENS = 384
REPLICAS = 16


def block_levels(rng, shape, split, low, top_value):
    gain = 1.0
    for axis_at, parts in split:
        heights = jax.random.uniform(jax.random.fold_in(jax.random.fold_in(rng, 6), axis_at), (parts,), jnp.float32, low / len(split), top_value / len(split))
        gain = gain * jnp.repeat(jnp.exp(heights), shape[axis_at] // parts).reshape((-1,) + (1,) * (len(shape) - 1 - axis_at))
    return gain


def scatter_about(own_key, dims, spread, limit, shards=(), held_as=jnp.bfloat16):
    drawn = spread * jax.random.normal(own_key, dims, jnp.float32)
    if shards:
        drawn = drawn * block_levels(own_key, dims, shards, -0.22, 0.18)
    return jnp.clip(drawn, -limit, limit).astype(held_as)


def setup_inputs(seed: int = 0) -> dict:
    splits = jax.random.split(jax.random.key(seed), 7)
    features = scatter_about(splits[0], (REPLICAS, TOKENS, D_IN), 1.0, 6.0, ((0, 16), (1, 2)))
    cotangent = scatter_about(splits[1], (REPLICAS, TOKENS, E), 1.0, 6.0, ((0, 16), (1, 2)))
    master = scatter_about(splits[2], (REPLICAS, D_IN, E), 0.05, 0.75, ((0, 16), (2, 2)), jnp.float32)
    moment = scatter_about(splits[3], (REPLICAS, D_IN, E), 0.5, 6.0, ((0, 16), (2, 2)))
    variance = jnp.clip(jnp.exp(math.log(1.0) - 2.9957323 * jax.random.uniform(splits[4], (REPLICAS, D_IN, E), jnp.float32) ** block_levels(splits[4], (REPLICAS, D_IN, E), ((0, 16), (2, 2)), -0.2, 0.2)), 0.05, 1.0)
    step_count = jax.random.randint(splits[5], (1,), 1, 25).astype(jnp.int32)
    return {"features": features, "cotangent": cotangent, "master": master, "moment": moment, "variance": variance, "step_count": step_count}


def head_gradient(tokens, weights, cotangent, heads_here):
    scale = D_IN ** (-0.5)
    query = jnp.dot(tokens, weights, preferred_element_type=jnp.float32) * scale
    count_rows = query.shape[0]
    shaped = query.reshape(count_rows, heads_here, HEAD)
    inverse = lax.rsqrt(lax.optimization_barrier(jnp.mean(shaped * shaped, axis=-1, keepdims=True)) + 1e-06)
    normed = shaped * inverse
    upstream = cotangent.astype(jnp.float32).reshape(count_rows, heads_here, HEAD)
    projected = lax.optimization_barrier(jnp.mean(upstream * normed, axis=-1, keepdims=True))
    dquery = (inverse * (upstream - normed * projected)).reshape(count_rows, heads_here * HEAD).astype(jnp.bfloat16)
    return lax.dot_general(tokens, dquery, (((0,), (0,)), ((), ())), preferred_element_type=jnp.float32)

def reference(features, cotangent, master, moment, variance, step_count):

    def one_replica(packed):
        tokens, upstream, weight = packed
        return head_gradient(tokens, weight.astype(jnp.bfloat16), upstream, HEADS) * D_IN ** (-0.5)
    grads = lax.map(one_replica, (features, cotangent, master))
    counter = step_count[0]
    power = counter.astype(jnp.float32)
    correct_first = 1.0 - jnp.power(jnp.float32(0.9), power)
    correct_second = 1.0 - jnp.power(jnp.float32(0.999), power)
    first = 0.9 * moment.astype(jnp.float32) + 0.1 * grads
    second = 0.999 * variance + 0.001 * grads * grads
    update = 0.1 * (first / correct_first / (jnp.sqrt(second / correct_second) + 1e-08) + 0.1 * master)
    fresh = master - update
    distance = jnp.left_shift(jnp.int32(1), counter % 4)
    return 0.5 * (fresh + jnp.roll(fresh, distance, axis=0))
```

```python
from functools import partial

import jax
import jax.numpy as jnp
from jax import lax
from jax.experimental import pallas as pl
from jax.experimental.pallas import tpu as pltpu
from jax.sharding import PartitionSpec as P

HEAD = 128
ROWS = 256
MESH = pl.DeviceIdType.MESH


def kernel(
    peers,
    count,
    distance,
    features,
    cotangent,
    master,
    moment,
    variance,
    scalars,
    mixed,
    tokens,
    flipped,
    upstream,
    dquery,
    params,
    first_in,
    second_in,
    outgoing,
    incoming,
    own_sem,
    load_sem,
    feature_send,
    feature_recv,
    column_send,
    column_recv,
    gossip_send,
    gossip_recv,
    store_sem,
):
    chunks, depth, _ = params.shape
    here = tokens.shape[1]
    scale = depth ** (-0.5)
    replica, me = lax.axis_index("replica"), lax.axis_index("fsdp")
    target = lax.rem(replica + distance, count)
    source = lax.rem(replica + count - distance, count)

    def columns(chunk):
        return pl.ds(pl.multiple_of(chunk * HEAD, HEAD), HEAD)

    def owned(chunk):
        return pltpu.make_async_copy(
            cotangent.at[0, :, columns(me * chunks + chunk)],
            upstream.at[chunk, 0],
            own_sem.at[1 + chunk],
        )

    def loads(chunk):
        return [
            pltpu.make_async_copy(
                whole.at[0, :, columns(chunk)], held.at[chunk], load_sem.at[at, chunk]
            )
            for at, (whole, held) in enumerate(
                ((master, params), (moment, first_in), (variance, second_in))
            )
        ]

    def features_to(step):
        return pltpu.make_async_remote_copy(
            src_ref=features.at[0],
            dst_ref=tokens.at[step],
            send_sem=feature_send.at[step],
            recv_sem=feature_recv.at[step],
            device_id={"fsdp": lax.rem(me + step, peers)},
            device_id_type=MESH,
        )

    def columns_to(step, chunk):
        peer = lax.rem(me + step, peers)
        return pltpu.make_async_remote_copy(
            src_ref=cotangent.at[0, :, columns(peer * chunks + chunk)],
            dst_ref=upstream.at[chunk, step],
            send_sem=column_send.at[step, chunk],
            recv_sem=column_recv.at[step, chunk],
            device_id={"fsdp": peer},
            device_id_type=MESH,
        )

    def gossip(chunk):
        return pltpu.make_async_remote_copy(
            src_ref=outgoing.at[chunk],
            dst_ref=incoming.at[chunk],
            send_sem=gossip_send.at[chunk],
            recv_sem=gossip_recv.at[chunk],
            device_id={"replica": target},
            device_id_type=MESH,
        )

    def stored(chunk):
        return pltpu.make_async_copy(
            params.at[chunk], mixed.at[0, :, columns(chunk)], store_sem.at[chunk]
        )

    barrier = pltpu.get_barrier_semaphore()
    for step in range(1, peers):
        pl.semaphore_signal(
            barrier, inc=1, device_id={"fsdp": lax.rem(me + step, peers)}, device_id_type=MESH
        )
    pl.semaphore_signal(barrier, inc=1, device_id={"replica": source}, device_id_type=MESH)
    own_features = pltpu.make_async_copy(features.at[0], tokens.at[0], own_sem.at[0])
    own_features.start()
    pl.semaphore_wait(barrier, peers)

    for step in range(1, peers):
        features_to(step).start()
    for step in range(1, peers):
        columns_to(step, 0).start()

    @pl.loop(0, chunks)
    def _(chunk):
        owned(chunk).start()
        for copy in loads(chunk):
            copy.start()

    def flip(step):
        @pl.loop(0, depth // ROWS)
        def _(block):
            rows = pl.ds(pl.multiple_of(block * ROWS, ROWS), ROWS)
            flipped[step, rows, :] = tokens[step, :, rows].T

    own_features.wait()
    flip(0)
    for step in range(1, peers):
        features_to(step).wait_recv()

        @pl.loop(1, chunks)
        def _(chunk):
            columns_to(step, chunk).start()

        flip(step)

    correct_first, correct_second = scalars[0], scalars[1]

    @pl.loop(0, chunks)
    def _(chunk):
        owned(chunk).wait()
        for copy in loads(chunk):
            copy.wait()
        for step in range(1, peers):
            columns_to(step, chunk).wait_recv()
        weights = params[chunk].astype(jnp.bfloat16)

        @pl.loop(0, peers)
        def _(step):
            query = jnp.dot(tokens[step], weights, preferred_element_type=jnp.float32) * scale
            inverse = lax.rsqrt(jnp.mean(query * query, axis=-1, keepdims=True) + 1e-06)
            normed = query * inverse
            cot = upstream[chunk, step].astype(jnp.float32)
            projected = jnp.mean(cot * normed, axis=-1, keepdims=True)
            dquery[step] = (inverse * (cot - normed * projected)).astype(jnp.bfloat16)

        @pl.loop(0, depth // ROWS)
        def _(block):
            rows = pl.ds(pl.multiple_of(block * ROWS, ROWS), ROWS)
            grads = jnp.dot(flipped[0, rows, :], dquery[0], preferred_element_type=jnp.float32)
            for step in range(1, peers):
                grads += jnp.dot(
                    flipped[step, rows, :], dquery[step], preferred_element_type=jnp.float32
                )
            grads = grads * scale
            param = params[chunk, rows, :]
            first = 0.9 * first_in[chunk, rows, :].astype(jnp.float32) + 0.1 * grads
            second = 0.999 * second_in[chunk, rows, :] + 0.001 * grads * grads
            update = 0.1 * (
                first * correct_first / (jnp.sqrt(second * correct_second) + 1e-08) + 0.1 * param
            )
            half = 0.5 * (param - update)
            params[chunk, rows, :] = half
            outgoing[chunk, rows, :] = half.astype(jnp.bfloat16)

        gossip(chunk).start()

    @pl.loop(0, chunks)
    def _(chunk):
        gossip(chunk).wait_recv()

        @pl.loop(0, depth // ROWS)
        def _(block):
            rows = pl.ds(pl.multiple_of(block * ROWS, ROWS), ROWS)
            params[chunk, rows, :] += incoming[chunk, rows, :].astype(jnp.float32)

        stored(chunk).start()

    for step in range(1, peers):
        features_to(step).wait_send()

    @pl.loop(0, chunks)
    def _(chunk):
        for step in range(1, peers):
            columns_to(step, chunk).wait_send()
        gossip(chunk).wait_send()
        stored(chunk).wait()


def updated(features, cotangent, master, moment, variance, scalars, peers, count, distance, which):
    _, here, depth = features.shape
    local = master.shape[2]
    chunks = local // HEAD
    dma = pltpu.SemaphoreType.DMA
    values = depth * local
    return pl.pallas_call(
        partial(kernel, peers, count, distance),
        out_shape=jax.ShapeDtypeStruct(master.shape, jnp.float32),
        in_specs=[pl.BlockSpec(memory_space=pl.ANY)] * 5
        + [pl.BlockSpec(memory_space=pltpu.SMEM)],
        out_specs=pl.BlockSpec(memory_space=pl.ANY),
        scratch_shapes=[
            pltpu.VMEM((peers, here, depth), jnp.bfloat16),
            pltpu.VMEM((peers, depth, here), jnp.bfloat16),
            pltpu.VMEM((chunks, peers, here, HEAD), jnp.bfloat16),
            pltpu.VMEM((peers, here, HEAD), jnp.bfloat16),
            pltpu.VMEM((chunks, depth, HEAD), jnp.float32),
            pltpu.VMEM((chunks, depth, HEAD), jnp.bfloat16),
            pltpu.VMEM((chunks, depth, HEAD), jnp.float32),
            pltpu.VMEM((chunks, depth, HEAD), jnp.bfloat16),
            pltpu.VMEM((chunks, depth, HEAD), jnp.bfloat16),
            dma((1 + chunks,)),
            dma((3, chunks)),
            dma((peers,)),
            dma((peers,)),
            dma((peers, chunks)),
            dma((peers, chunks)),
            dma((chunks,)),
            dma((chunks,)),
            dma((chunks,)),
        ],
        compiler_params=pltpu.CompilerParams(
            collective_id=which, has_side_effects=True, vmem_limit_bytes=52 * 1024 * 1024
        ),
        cost_estimate=pl.CostEstimate(
            flops=4 * peers * here * values, bytes_accessed=18 * values, transcendentals=values
        ),
        name=f"step_{distance}",
    )(features, cotangent, master, moment, variance, scalars)


def body(peers, count, features, cotangent, master, moment, variance, step_count):
    counter = step_count[0]
    power = counter.astype(jnp.float32)
    correct_first = 1.0 - jnp.power(jnp.float32(0.9), power)
    correct_second = 1.0 - jnp.power(jnp.float32(0.999), power)
    scalars = jnp.stack([1.0 / correct_first, 1.0 / correct_second])
    return lax.switch(
        counter % 4,
        [
            partial(updated, peers=peers, count=count, distance=1 << level, which=level)
            for level in range(4)
        ],
        features,
        cotangent,
        master,
        moment,
        variance,
        scalars,
    )


def solution(mesh):
    placed = (
        P("replica", "fsdp", None),
        P("replica", "fsdp", None),
        P("replica", None, "fsdp"),
        P("replica", None, "fsdp"),
        P("replica", None, "fsdp"),
        P(),
    )
    return jax.shard_map(
        partial(body, mesh.shape["fsdp"], mesh.shape["replica"]),
        mesh=mesh,
        in_specs=placed,
        out_specs=P("replica", None, "fsdp"),
        check_vma=False,
    )
```

```python
from functools import partial

import jax
import jax.numpy as jnp
from jax import lax
from jax.experimental import pallas as pl
from jax.experimental.pallas import tpu as pltpu
from jax.sharding import PartitionSpec as P

HEAD = 128
ROWS = 256
PIECES = 4
PARTS = 2
MESH = pl.DeviceIdType.MESH


def kernel(
    peers,
    count,
    distance,
    features,
    cotangent,
    master,
    moment,
    variance,
    scalars,
    mixed,
    tokens,
    flipped,
    upstream,
    dquery,
    params,
    first_in,
    second_in,
    outgoing,
    incoming,
    own_sem,
    go_sem,
    load_sem,
    feature_send,
    feature_recv,
    column_send,
    column_recv,
    gossip_send,
    gossip_recv,
    store_sem,
):
    chunks, depth, _ = params.shape
    scale = depth ** (-0.5)
    replica, me = lax.axis_index("replica"), lax.axis_index("fsdp")
    target = lax.rem(replica + distance, count)
    source = lax.rem(replica + count - distance, count)
    odd = lax.rem(replica, 2)
    partner = replica + 1 - 2 * odd
    leads = odd == distance % 2

    def span(at, parts):
        size = depth // parts
        return pl.ds(pl.multiple_of(at * size, size), size)

    def columns(chunk):
        return pl.ds(pl.multiple_of(chunk * HEAD, HEAD), HEAD)

    def owned(chunk):
        return pltpu.make_async_copy(
            cotangent.at[0, :, columns(me * chunks + chunk)],
            upstream.at[chunk, 0],
            own_sem.at[1 + chunk],
        )

    def loads(chunk):
        return [
            pltpu.make_async_copy(
                whole.at[0, :, columns(chunk)], held.at[chunk], load_sem.at[at, chunk]
            )
            for at, (whole, held) in enumerate(
                ((master, params), (moment, first_in), (variance, second_in))
            )
        ]

    def features_to(step, piece):
        return pltpu.make_async_remote_copy(
            src_ref=features.at[0, :, span(piece, PIECES)],
            dst_ref=tokens.at[step, :, span(piece, PIECES)],
            send_sem=feature_send.at[step, piece],
            recv_sem=feature_recv.at[step, piece],
            device_id={"fsdp": lax.rem(me + step, peers)},
            device_id_type=MESH,
        )

    def columns_to(step, chunk):
        peer = lax.rem(me + step, peers)
        return pltpu.make_async_remote_copy(
            src_ref=cotangent.at[0, :, columns(peer * chunks + chunk)],
            dst_ref=upstream.at[chunk, step],
            send_sem=column_send.at[step, chunk],
            recv_sem=column_recv.at[step, chunk],
            device_id={"fsdp": peer},
            device_id_type=MESH,
        )

    def gossip(chunk, part):
        return pltpu.make_async_remote_copy(
            src_ref=outgoing.at[chunk, span(part, PARTS)],
            dst_ref=incoming.at[chunk, span(part, PARTS)],
            send_sem=gossip_send.at[chunk, part],
            recv_sem=gossip_recv.at[chunk, part],
            device_id={"replica": target},
            device_id_type=MESH,
        )

    def stored(chunk, part):
        return pltpu.make_async_copy(
            params.at[chunk, span(part, PARTS)],
            mixed.at[0, span(part, PARTS), columns(chunk)],
            store_sem.at[chunk, part],
        )

    def send_features():
        @pl.loop(1, peers)
        def _(step):
            for piece in range(PIECES):
                features_to(step, piece).start()
            columns_to(step, 0).start()

    def features_left(pieces):
        @pl.loop(1, peers)
        def _(step):
            for piece in pieces:
                features_to(step, piece).wait_send()

    barrier = pltpu.get_barrier_semaphore()
    for step in range(1, peers):
        pl.semaphore_signal(
            barrier, inc=1, device_id={"fsdp": lax.rem(me + step, peers)}, device_id_type=MESH
        )
    pl.semaphore_signal(barrier, inc=1, device_id={"replica": source}, device_id_type=MESH)
    pl.semaphore_signal(barrier, inc=1, device_id={"replica": partner}, device_id_type=MESH)
    own_features = pltpu.make_async_copy(features.at[0], tokens.at[0], own_sem.at[0])
    own_features.start()
    pl.semaphore_wait(barrier, peers + 1)

    @pl.when(leads)
    def _():
        send_features()

    @pl.loop(0, chunks)
    def _(chunk):
        owned(chunk).start()
        for copy in loads(chunk):
            copy.start()

    def flip(step, piece):
        blocks = depth // PIECES // ROWS

        @pl.loop(0, blocks)
        def _(block):
            at = (piece * blocks + block) * ROWS
            rows = pl.ds(pl.multiple_of(at, ROWS), ROWS)
            flipped[step, rows, :] = tokens[step, :, rows].T

    own_features.wait()
    for piece in range(PIECES):
        flip(0, piece)

    @pl.when(leads)
    def _():
        features_left(range(PIECES - 1))
        pl.semaphore_signal(go_sem, inc=1, device_id={"replica": partner}, device_id_type=MESH)

    @pl.when(jnp.logical_not(leads))
    def _():
        pl.semaphore_wait(go_sem, 1)
        send_features()

    @pl.loop(1, peers)
    def _(step):
        for piece in range(PIECES):
            features_to(step, piece).wait_recv()
            flip(step, piece)

    @pl.loop(1, chunks)
    def _(chunk):
        for step in range(1, peers):
            columns_to(step, chunk).start()

    correct_first, correct_second = scalars[0], scalars[1]

    @pl.loop(0, chunks)
    def _(chunk):
        owned(chunk).wait()
        for copy in loads(chunk):
            copy.wait()
        for step in range(1, peers):
            columns_to(step, chunk).wait_recv()
        weights = params[chunk].astype(jnp.bfloat16)

        @pl.loop(0, peers)
        def _(step):
            query = jnp.dot(tokens[step], weights, preferred_element_type=jnp.float32) * scale
            inverse = lax.rsqrt(jnp.mean(query * query, axis=-1, keepdims=True) + 1e-06)
            normed = query * inverse
            cot = upstream[chunk, step].astype(jnp.float32)
            projected = jnp.mean(cot * normed, axis=-1, keepdims=True)
            dquery[step] = (inverse * (cot - normed * projected)).astype(jnp.bfloat16)

        def revise(block):
            rows = pl.ds(pl.multiple_of(block * ROWS, ROWS), ROWS)
            grads = jnp.dot(flipped[0, rows, :], dquery[0], preferred_element_type=jnp.float32)
            for step in range(1, peers):
                grads += jnp.dot(
                    flipped[step, rows, :], dquery[step], preferred_element_type=jnp.float32
                )
            grads = grads * scale
            param = params[chunk, rows, :]
            first = 0.9 * first_in[chunk, rows, :].astype(jnp.float32) + 0.1 * grads
            second = 0.999 * second_in[chunk, rows, :] + 0.001 * grads * grads
            update = 0.1 * (
                first * correct_first / (jnp.sqrt(second * correct_second) + 1e-08) + 0.1 * param
            )
            half = 0.5 * (param - update)
            params[chunk, rows, :] = half
            outgoing[chunk, rows, :] = half.astype(jnp.bfloat16)

        for part in range(PARTS):
            blocks = depth // PARTS // ROWS
            pl.loop(part * blocks, (part + 1) * blocks)(revise)
            gossip(chunk, part).start()

    @pl.loop(0, chunks)
    def _(chunk):
        for part in range(PARTS):
            gossip(chunk, part).wait_recv()
            rows = span(part, PARTS)
            params[chunk, rows, :] += incoming[chunk, rows, :].astype(jnp.float32)
            stored(chunk, part).start()

    features_left([PIECES - 1])

    @pl.when(jnp.logical_not(leads))
    def _():
        features_left(range(PIECES - 1))

    @pl.loop(0, chunks)
    def _(chunk):
        for step in range(1, peers):
            columns_to(step, chunk).wait_send()
        for part in range(PARTS):
            gossip(chunk, part).wait_send()
            stored(chunk, part).wait()


def updated(features, cotangent, master, moment, variance, scalars, peers, count, distance, which):
    _, here, depth = features.shape
    local = master.shape[2]
    chunks = local // HEAD
    dma = pltpu.SemaphoreType.DMA
    values = depth * local
    return pl.pallas_call(
        partial(kernel, peers, count, distance),
        out_shape=jax.ShapeDtypeStruct(master.shape, jnp.float32),
        in_specs=[pl.BlockSpec(memory_space=pl.ANY)] * 5
        + [pl.BlockSpec(memory_space=pltpu.SMEM)],
        out_specs=pl.BlockSpec(memory_space=pl.ANY),
        scratch_shapes=[
            pltpu.VMEM((peers, here, depth), jnp.bfloat16),
            pltpu.VMEM((peers, depth, here), jnp.bfloat16),
            pltpu.VMEM((chunks, peers, here, HEAD), jnp.bfloat16),
            pltpu.VMEM((peers, here, HEAD), jnp.bfloat16),
            pltpu.VMEM((chunks, depth, HEAD), jnp.float32),
            pltpu.VMEM((chunks, depth, HEAD), jnp.bfloat16),
            pltpu.VMEM((chunks, depth, HEAD), jnp.float32),
            pltpu.VMEM((chunks, depth, HEAD), jnp.bfloat16),
            pltpu.VMEM((chunks, depth, HEAD), jnp.bfloat16),
            dma((1 + chunks,)),
            pltpu.SemaphoreType.REGULAR,
            dma((3, chunks)),
            dma((peers, PIECES)),
            dma((peers, PIECES)),
            dma((peers, chunks)),
            dma((peers, chunks)),
            dma((chunks, PARTS)),
            dma((chunks, PARTS)),
            dma((chunks, PARTS)),
        ],
        compiler_params=pltpu.CompilerParams(
            collective_id=which, has_side_effects=True, vmem_limit_bytes=52 * 1024 * 1024
        ),
        cost_estimate=pl.CostEstimate(
            flops=4 * peers * here * values, bytes_accessed=18 * values, transcendentals=values
        ),
        name=f"step_{distance}",
    )(features, cotangent, master, moment, variance, scalars)


def body(peers, count, features, cotangent, master, moment, variance, step_count):
    counter = step_count[0]
    power = counter.astype(jnp.float32)
    correct_first = 1.0 - jnp.power(jnp.float32(0.9), power)
    correct_second = 1.0 - jnp.power(jnp.float32(0.999), power)
    scalars = jnp.stack([1.0 / correct_first, 1.0 / correct_second])
    return lax.switch(
        counter % 4,
        [
            partial(updated, peers=peers, count=count, distance=1 << level, which=level)
            for level in range(4)
        ],
        features,
        cotangent,
        master,
        moment,
        variance,
        scalars,
    )


def solution(mesh):
    placed = (
        P("replica", "fsdp", None),
        P("replica", "fsdp", None),
        P("replica", None, "fsdp"),
        P("replica", None, "fsdp"),
        P("replica", None, "fsdp"),
        P(),
    )
    return jax.shard_map(
        partial(body, mesh.shape["fsdp"], mesh.shape["replica"]),
        mesh=mesh,
        in_specs=placed,
        out_specs=P("replica", None, "fsdp"),
        check_vma=False,
    )
```

```python
from functools import partial

import jax
import jax.numpy as jnp
from jax import lax
from jax.experimental import pallas as pl
from jax.experimental.pallas import tpu as pltpu
from jax.sharding import PartitionSpec as P

HEAD = 128
ROWS = 256
STRIP = 32
PIECES = 4
PARTS = 2
MESH = pl.DeviceIdType.MESH


def kernel(
    peers,
    count,
    distance,
    features,
    cotangent,
    master,
    moment,
    variance,
    scalars,
    mixed,
    tokens,
    flipped,
    upstream,
    dquery,
    grads,
    params,
    first_in,
    second_in,
    outgoing,
    incoming,
    own_sem,
    go_sem,
    load_sem,
    feature_send,
    feature_recv,
    column_send,
    column_recv,
    gossip_send,
    gossip_recv,
    store_sem,
):
    chunks, depth, _ = params.shape
    scale = depth ** (-0.5)
    replica, me = lax.axis_index("replica"), lax.axis_index("fsdp")
    target = lax.rem(replica + distance, count)
    source = lax.rem(replica + count - distance, count)
    odd = lax.rem(replica, 2)
    partner = replica + 1 - 2 * odd
    leads = odd == distance % 2

    def span(at, parts):
        size = depth // parts
        return pl.ds(pl.multiple_of(at * size, size), size)

    def columns(chunk):
        return pl.ds(pl.multiple_of(chunk * HEAD, HEAD), HEAD)

    def owned(chunk):
        return pltpu.make_async_copy(
            cotangent.at[0, :, columns(me * chunks + chunk)],
            upstream.at[chunk, 0],
            own_sem.at[1 + chunk],
        )

    def loads(chunk):
        return [
            pltpu.make_async_copy(
                whole.at[0, :, columns(chunk)], held.at[chunk], load_sem.at[at, chunk]
            )
            for at, (whole, held) in enumerate(
                ((master, params), (moment, first_in), (variance, second_in))
            )
        ]

    def features_to(step, piece):
        return pltpu.make_async_remote_copy(
            src_ref=features.at[0, :, span(piece, PIECES)],
            dst_ref=tokens.at[step, :, span(piece, PIECES)],
            send_sem=feature_send.at[step, piece],
            recv_sem=feature_recv.at[step, piece],
            device_id={"fsdp": lax.rem(me + step, peers)},
            device_id_type=MESH,
        )

    def columns_to(step, chunk):
        peer = lax.rem(me + step, peers)
        return pltpu.make_async_remote_copy(
            src_ref=cotangent.at[0, :, columns(peer * chunks + chunk)],
            dst_ref=upstream.at[chunk, step],
            send_sem=column_send.at[step, chunk],
            recv_sem=column_recv.at[step, chunk],
            device_id={"fsdp": peer},
            device_id_type=MESH,
        )

    def gossip(chunk, part):
        return pltpu.make_async_remote_copy(
            src_ref=outgoing.at[chunk, span(part, PARTS)],
            dst_ref=incoming.at[chunk, span(part, PARTS)],
            send_sem=gossip_send.at[chunk, part],
            recv_sem=gossip_recv.at[chunk, part],
            device_id={"replica": target},
            device_id_type=MESH,
        )

    def stored(chunk, part):
        return pltpu.make_async_copy(
            params.at[chunk, span(part, PARTS)],
            mixed.at[0, span(part, PARTS), columns(chunk)],
            store_sem.at[chunk, part],
        )

    def send_features():
        @pl.loop(1, peers)
        def _(step):
            for piece in range(PIECES):
                features_to(step, piece).start()
            columns_to(step, 0).start()

    def features_left(pieces):
        @pl.loop(1, peers)
        def _(step):
            for piece in pieces:
                features_to(step, piece).wait_send()

    barrier = pltpu.get_barrier_semaphore()
    for step in range(1, peers):
        pl.semaphore_signal(
            barrier, inc=1, device_id={"fsdp": lax.rem(me + step, peers)}, device_id_type=MESH
        )
    pl.semaphore_signal(barrier, inc=1, device_id={"replica": source}, device_id_type=MESH)
    pl.semaphore_signal(barrier, inc=1, device_id={"replica": partner}, device_id_type=MESH)
    own_features = pltpu.make_async_copy(features.at[0], tokens.at[0], own_sem.at[0])
    own_features.start()

    def load(chunk):
        owned(chunk).start()
        for copy in loads(chunk):
            copy.start()

    load(0)
    pl.semaphore_wait(barrier, peers + 1)

    @pl.when(leads)
    def _():
        send_features()

    pl.loop(1, chunks)(load)

    def flip(step, piece):
        blocks = depth // PIECES // ROWS

        @pl.loop(0, blocks)
        def _(block):
            at = (piece * blocks + block) * ROWS
            rows = pl.ds(pl.multiple_of(at, ROWS), ROWS)
            flipped[step, rows, :] = tokens[step, :, rows].T

    own_features.wait()
    for piece in range(PIECES):
        flip(0, piece)

    @pl.when(leads)
    def _():
        features_left(range(PIECES - 1))
        pl.semaphore_signal(go_sem, inc=1, device_id={"replica": partner}, device_id_type=MESH)

    @pl.when(jnp.logical_not(leads))
    def _():
        pl.semaphore_wait(go_sem, 1)
        send_features()

    @pl.loop(1, peers)
    def _(step):
        for piece in range(PIECES):
            features_to(step, piece).wait_recv()
            flip(step, piece)

    def send_columns(chunk):
        @pl.loop(1, peers)
        def _(step):
            columns_to(step, chunk).start()

    for chunk in range(1, min(3, chunks)):
        send_columns(chunk)

    of_variance, of_square, of_moment, of_grad = [scalars[at] for at in range(4)]

    @pl.loop(0, chunks)
    def _(chunk):
        owned(chunk).wait()
        for copy in loads(chunk):
            copy.wait()
        for step in range(1, peers):
            columns_to(step, chunk).wait_recv()

        @pl.when(chunk + 3 < chunks)
        def _():
            send_columns(chunk + 3)

        weights = params[chunk].astype(jnp.bfloat16)

        @pl.loop(0, peers)
        def _(step):
            query = jnp.dot(tokens[step], weights, preferred_element_type=jnp.float32) * scale
            inverse = lax.rsqrt(jnp.mean(query * query, axis=-1, keepdims=True) + 1e-06)
            normed = query * inverse
            cot = upstream[chunk, step].astype(jnp.float32)
            projected = jnp.mean(cot * normed, axis=-1, keepdims=True)
            dquery[step] = (inverse * (cot - normed * projected)).astype(jnp.bfloat16)

        def revise(block):
            rows = pl.ds(pl.multiple_of(block * ROWS, ROWS), ROWS)
            total = jnp.dot(flipped[0, rows, :], dquery[0], preferred_element_type=jnp.float32)
            for step in range(1, peers):
                total += jnp.dot(
                    flipped[step, rows, :], dquery[step], preferred_element_type=jnp.float32
                )
            grads[...] = total
            for strip in range(ROWS // STRIP):
                rows = pl.ds(pl.multiple_of(block * ROWS + strip * STRIP, STRIP), STRIP)
                grad = grads[pl.ds(strip * STRIP, STRIP), :]
                moment_here = first_in[chunk, rows, :].astype(jnp.float32)
                square = of_variance * second_in[chunk, rows, :] + of_square * (grad * grad)
                root = lax.rsqrt(square)
                bottom = square * root + 1e-08
                inverse = root * (2.0 - bottom * root)
                top = of_moment * moment_here + of_grad * grad
                half = 0.495 * params[chunk, rows, :] - top * inverse
                params[chunk, rows, :] = half
                outgoing[chunk, rows, :] = half.astype(jnp.bfloat16)

        for part in range(PARTS):
            blocks = depth // PARTS // ROWS
            pl.loop(part * blocks, (part + 1) * blocks)(revise)
            gossip(chunk, part).start()

    @pl.loop(0, chunks)
    def _(chunk):
        for part in range(PARTS):
            gossip(chunk, part).wait_recv()
            rows = span(part, PARTS)
            params[chunk, rows, :] += incoming[chunk, rows, :].astype(jnp.float32)
            stored(chunk, part).start()

    features_left([PIECES - 1])

    @pl.when(jnp.logical_not(leads))
    def _():
        features_left(range(PIECES - 1))

    @pl.loop(0, chunks)
    def _(chunk):
        for step in range(1, peers):
            columns_to(step, chunk).wait_send()
        for part in range(PARTS):
            gossip(chunk, part).wait_send()
            stored(chunk, part).wait()


def updated(features, cotangent, master, moment, variance, scalars, peers, count, distance, which):
    _, here, depth = features.shape
    local = master.shape[2]
    chunks = local // HEAD
    dma = pltpu.SemaphoreType.DMA
    values = depth * local
    return pl.pallas_call(
        partial(kernel, peers, count, distance),
        out_shape=jax.ShapeDtypeStruct(master.shape, jnp.float32),
        in_specs=[pl.BlockSpec(memory_space=pl.ANY)] * 5
        + [pl.BlockSpec(memory_space=pltpu.SMEM)],
        out_specs=pl.BlockSpec(memory_space=pl.ANY),
        scratch_shapes=[
            pltpu.VMEM((peers, here, depth), jnp.bfloat16),
            pltpu.VMEM((peers, depth, here), jnp.bfloat16),
            pltpu.VMEM((chunks, peers, here, HEAD), jnp.bfloat16),
            pltpu.VMEM((peers, here, HEAD), jnp.bfloat16),
            pltpu.VMEM((ROWS, HEAD), jnp.float32),
            pltpu.VMEM((chunks, depth, HEAD), jnp.float32),
            pltpu.VMEM((chunks, depth, HEAD), jnp.bfloat16),
            pltpu.VMEM((chunks, depth, HEAD), jnp.float32),
            pltpu.VMEM((chunks, depth, HEAD), jnp.bfloat16),
            pltpu.VMEM((chunks, depth, HEAD), jnp.bfloat16),
            dma((1 + chunks,)),
            pltpu.SemaphoreType.REGULAR,
            dma((3, chunks)),
            dma((peers, PIECES)),
            dma((peers, PIECES)),
            dma((peers, chunks)),
            dma((peers, chunks)),
            dma((chunks, PARTS)),
            dma((chunks, PARTS)),
            dma((chunks, PARTS)),
        ],
        compiler_params=pltpu.CompilerParams(
            collective_id=which, has_side_effects=True, vmem_limit_bytes=52 * 1024 * 1024
        ),
        cost_estimate=pl.CostEstimate(
            flops=4 * peers * here * values, bytes_accessed=18 * values, transcendentals=values
        ),
        name=f"step_{distance}",
    )(features, cotangent, master, moment, variance, scalars)


def body(peers, count, features, cotangent, master, moment, variance, step_count):
    counter = step_count[0]
    power = counter.astype(jnp.float32)
    correct_first = 1.0 - jnp.power(jnp.float32(0.9), power)
    correct_second = 1.0 - jnp.power(jnp.float32(0.999), power)
    scale = master.shape[1] ** (-0.5)
    scalars = jnp.stack(
        [
            0.999 / correct_second,
            0.001 * scale * scale / correct_second,
            0.05 * 0.9 / correct_first,
            0.05 * 0.1 * scale / correct_first,
        ]
    )
    return lax.switch(
        counter % 4,
        [
            partial(updated, peers=peers, count=count, distance=1 << level, which=level)
            for level in range(4)
        ],
        features,
        cotangent,
        master,
        moment,
        variance,
        scalars,
    )


def solution(mesh):
    placed = (
        P("replica", "fsdp", None),
        P("replica", "fsdp", None),
        P("replica", None, "fsdp"),
        P("replica", None, "fsdp"),
        P("replica", None, "fsdp"),
        P(),
    )
    return jax.shard_map(
        partial(body, mesh.shape["fsdp"], mesh.shape["replica"]),
        mesh=mesh,
        in_specs=placed,
        out_specs=P("replica", None, "fsdp"),
        check_vma=False,
    )
```

```python
from functools import partial

import jax
import jax.numpy as jnp
from jax import lax
from jax.experimental import pallas as pl
from jax.experimental.pallas import tpu as pltpu
from jax.sharding import PartitionSpec as P

HEAD = 128
ROWS = 256
STRIP = 32
PIECES = 4
PARTS = 4
MESH = pl.DeviceIdType.MESH


def kernel(
    peers,
    count,
    distance,
    features,
    cotangent,
    master,
    moment,
    variance,
    scalars,
    mixed,
    tokens,
    flipped,
    upstream,
    dquery,
    grads,
    params,
    first_in,
    second_in,
    outgoing,
    incoming,
    own_sem,
    go_sem,
    load_sem,
    feature_send,
    feature_recv,
    column_send,
    column_recv,
    gossip_send,
    gossip_recv,
    store_sem,
):
    chunks, depth, _ = params.shape
    scale = depth ** (-0.5)
    replica, me = lax.axis_index("replica"), lax.axis_index("fsdp")
    target = lax.rem(replica + distance, count)
    source = lax.rem(replica + count - distance, count)
    odd = lax.rem(replica, 2)
    partner = replica + 1 - 2 * odd
    leads = odd == distance % 2

    def span(at, parts):
        size = depth // parts
        return pl.ds(pl.multiple_of(at * size, size), size)

    def columns(chunk):
        return pl.ds(pl.multiple_of(chunk * HEAD, HEAD), HEAD)

    def owned(chunk):
        return pltpu.make_async_copy(
            cotangent.at[0, :, columns(me * chunks + chunk)],
            upstream.at[chunk, 0],
            own_sem.at[1 + chunk],
        )

    def loads(chunk):
        return [
            pltpu.make_async_copy(
                whole.at[0, :, columns(chunk)], held.at[chunk], load_sem.at[at, chunk]
            )
            for at, (whole, held) in enumerate(
                ((master, params), (moment, first_in), (variance, second_in))
            )
        ]

    def features_to(step, piece):
        return pltpu.make_async_remote_copy(
            src_ref=features.at[0, :, span(piece, PIECES)],
            dst_ref=tokens.at[step, :, span(piece, PIECES)],
            send_sem=feature_send.at[step, piece],
            recv_sem=feature_recv.at[step, piece],
            device_id={"fsdp": lax.rem(me + step, peers)},
            device_id_type=MESH,
        )

    def columns_to(step, chunk):
        peer = lax.rem(me + step, peers)
        return pltpu.make_async_remote_copy(
            src_ref=cotangent.at[0, :, columns(peer * chunks + chunk)],
            dst_ref=upstream.at[chunk, step],
            send_sem=column_send.at[step, chunk],
            recv_sem=column_recv.at[step, chunk],
            device_id={"fsdp": peer},
            device_id_type=MESH,
        )

    def gossip(chunk, part):
        return pltpu.make_async_remote_copy(
            src_ref=outgoing.at[chunk, span(part, PARTS)],
            dst_ref=incoming.at[chunk, span(part, PARTS)],
            send_sem=gossip_send.at[chunk, part],
            recv_sem=gossip_recv.at[chunk, part],
            device_id={"replica": target},
            device_id_type=MESH,
        )

    def stored(chunk, part):
        return pltpu.make_async_copy(
            params.at[chunk, span(part, PARTS)],
            mixed.at[0, span(part, PARTS), columns(chunk)],
            store_sem.at[chunk, part],
        )

    def send_features():
        @pl.loop(1, peers)
        def _(step):
            for piece in range(PIECES):
                features_to(step, piece).start()
            columns_to(step, 0).start()

    def features_left(pieces):
        @pl.loop(1, peers)
        def _(step):
            for piece in pieces:
                features_to(step, piece).wait_send()

    barrier = pltpu.get_barrier_semaphore()
    for step in range(1, peers):
        pl.semaphore_signal(
            barrier, inc=1, device_id={"fsdp": lax.rem(me + step, peers)}, device_id_type=MESH
        )
    pl.semaphore_signal(barrier, inc=1, device_id={"replica": source}, device_id_type=MESH)
    pl.semaphore_signal(barrier, inc=1, device_id={"replica": partner}, device_id_type=MESH)
    own_features = pltpu.make_async_copy(features.at[0], tokens.at[0], own_sem.at[0])
    own_features.start()

    def load(chunk):
        owned(chunk).start()
        for copy in loads(chunk):
            copy.start()

    load(0)
    pl.semaphore_wait(barrier, peers + 1)

    @pl.when(leads)
    def _():
        send_features()

    pl.loop(1, chunks)(load)

    def flip(step, piece):
        blocks = depth // PIECES // ROWS

        @pl.loop(0, blocks)
        def _(block):
            at = (piece * blocks + block) * ROWS
            rows = pl.ds(pl.multiple_of(at, ROWS), ROWS)
            flipped[step, rows, :] = tokens[step, :, rows].T

    def arrived(chunk):
        owned(chunk).wait()
        for copy in loads(chunk):
            copy.wait()

    def weights_of(chunk):
        return params[chunk].astype(jnp.bfloat16)

    def backward(chunk, step, weights):
        query = jnp.dot(tokens[step], weights, preferred_element_type=jnp.float32) * scale
        inverse = lax.rsqrt(jnp.mean(query * query, axis=-1, keepdims=True) + 1e-06)
        normed = query * inverse
        cot = upstream[chunk, step].astype(jnp.float32)
        projected = jnp.mean(cot * normed, axis=-1, keepdims=True)
        dquery[step] = (inverse * (cot - normed * projected)).astype(jnp.bfloat16)

    own_features.wait()
    for piece in range(PIECES):
        flip(0, piece)
    arrived(0)
    backward(0, 0, weights_of(0))

    @pl.when(leads)
    def _():
        features_left(range(PIECES - 1))
        pl.semaphore_signal(go_sem, inc=1, device_id={"replica": partner}, device_id_type=MESH)

    @pl.when(jnp.logical_not(leads))
    def _():
        pl.semaphore_wait(go_sem, 1)
        send_features()

    @pl.loop(1, peers)
    def _(step):
        for piece in range(PIECES):
            features_to(step, piece).wait_recv()
            flip(step, piece)

    def send_columns(chunk):
        @pl.loop(1, peers)
        def _(step):
            columns_to(step, chunk).start()

    for chunk in range(1, min(3, chunks)):
        send_columns(chunk)

    of_variance, of_square, of_moment, of_grad = [scalars[at] for at in range(4)]

    def received(chunk, weights):
        @pl.loop(1, peers)
        def _(step):
            columns_to(step, chunk).wait_recv()
            backward(chunk, step, weights)

    def update(chunk):
        def revise(block):
            rows = pl.ds(pl.multiple_of(block * ROWS, ROWS), ROWS)
            total = jnp.dot(flipped[0, rows, :], dquery[0], preferred_element_type=jnp.float32)
            for step in range(1, peers):
                total += jnp.dot(
                    flipped[step, rows, :], dquery[step], preferred_element_type=jnp.float32
                )
            grads[...] = total
            for strip in range(ROWS // STRIP):
                rows = pl.ds(pl.multiple_of(block * ROWS + strip * STRIP, STRIP), STRIP)
                grad = grads[pl.ds(strip * STRIP, STRIP), :]
                moment_here = first_in[chunk, rows, :].astype(jnp.float32)
                square = of_variance * second_in[chunk, rows, :] + of_square * (grad * grad)
                root = lax.rsqrt(square)
                bottom = square * root + 1e-08
                inverse = root * (2.0 - bottom * root)
                top = of_moment * moment_here + of_grad * grad
                half = 0.495 * params[chunk, rows, :] - top * inverse
                params[chunk, rows, :] = half
                outgoing[chunk, rows, :] = half.astype(jnp.bfloat16)

        @pl.loop(0, PARTS)
        def _(part):
            blocks = depth // PARTS // ROWS

            @pl.loop(0, blocks)
            def _(block):
                revise(part * blocks + block)

            gossip(chunk, part).start()

    @pl.loop(0, chunks)
    def _(chunk):
        @pl.when(chunk > 0)
        def _():
            arrived(chunk)
            backward(chunk, 0, weights_of(chunk))

        @pl.when(chunk + 3 < chunks)
        def _():
            send_columns(chunk + 3)

        received(chunk, weights_of(chunk))
        update(chunk)

    @pl.loop(0, chunks)
    def _(chunk):
        @pl.loop(0, PARTS)
        def _(part):
            gossip(chunk, part).wait_recv()
            rows = span(part, PARTS)
            params[chunk, rows, :] += incoming[chunk, rows, :].astype(jnp.float32)
            stored(chunk, part).start()

    features_left([PIECES - 1])

    @pl.when(jnp.logical_not(leads))
    def _():
        features_left(range(PIECES - 1))

    @pl.loop(0, chunks)
    def _(chunk):
        for step in range(1, peers):
            columns_to(step, chunk).wait_send()
        for part in range(PARTS):
            gossip(chunk, part).wait_send()
            stored(chunk, part).wait()


def updated(features, cotangent, master, moment, variance, scalars, peers, count, distance, which):
    _, here, depth = features.shape
    local = master.shape[2]
    chunks = local // HEAD
    dma = pltpu.SemaphoreType.DMA
    values = depth * local
    return pl.pallas_call(
        partial(kernel, peers, count, distance),
        out_shape=jax.ShapeDtypeStruct(master.shape, jnp.float32),
        in_specs=[pl.BlockSpec(memory_space=pl.ANY)] * 5
        + [pl.BlockSpec(memory_space=pltpu.SMEM)],
        out_specs=pl.BlockSpec(memory_space=pl.ANY),
        scratch_shapes=[
            pltpu.VMEM((peers, here, depth), jnp.bfloat16),
            pltpu.VMEM((peers, depth, here), jnp.bfloat16),
            pltpu.VMEM((chunks, peers, here, HEAD), jnp.bfloat16),
            pltpu.VMEM((peers, here, HEAD), jnp.bfloat16),
            pltpu.VMEM((ROWS, HEAD), jnp.float32),
            pltpu.VMEM((chunks, depth, HEAD), jnp.float32),
            pltpu.VMEM((chunks, depth, HEAD), jnp.bfloat16),
            pltpu.VMEM((chunks, depth, HEAD), jnp.float32),
            pltpu.VMEM((chunks, depth, HEAD), jnp.bfloat16),
            pltpu.VMEM((chunks, depth, HEAD), jnp.bfloat16),
            dma((1 + chunks,)),
            pltpu.SemaphoreType.REGULAR,
            dma((3, chunks)),
            dma((peers, PIECES)),
            dma((peers, PIECES)),
            dma((peers, chunks)),
            dma((peers, chunks)),
            dma((chunks, PARTS)),
            dma((chunks, PARTS)),
            dma((chunks, PARTS)),
        ],
        compiler_params=pltpu.CompilerParams(
            collective_id=which, has_side_effects=True, vmem_limit_bytes=52 * 1024 * 1024
        ),
        cost_estimate=pl.CostEstimate(
            flops=4 * peers * here * values, bytes_accessed=18 * values, transcendentals=values
        ),
        name=f"step_{distance}",
    )(features, cotangent, master, moment, variance, scalars)


def body(peers, count, features, cotangent, master, moment, variance, step_count):
    counter = step_count[0]
    power = counter.astype(jnp.float32)
    correct_first = 1.0 - jnp.power(jnp.float32(0.9), power)
    correct_second = 1.0 - jnp.power(jnp.float32(0.999), power)
    scale = master.shape[1] ** (-0.5)
    scalars = jnp.stack(
        [
            0.999 / correct_second,
            0.001 * scale * scale / correct_second,
            0.05 * 0.9 / correct_first,
            0.05 * 0.1 * scale / correct_first,
        ]
    )
    return lax.switch(
        counter % 4,
        [
            partial(updated, peers=peers, count=count, distance=1 << level, which=level)
            for level in range(4)
        ],
        features,
        cotangent,
        master,
        moment,
        variance,
        scalars,
    )


def solution(mesh):
    placed = (
        P("replica", "fsdp", None),
        P("replica", "fsdp", None),
        P("replica", None, "fsdp"),
        P("replica", None, "fsdp"),
        P("replica", None, "fsdp"),
        P(),
    )
    return jax.shard_map(
        partial(body, mesh.shape["fsdp"], mesh.shape["replica"]),
        mesh=mesh,
        in_specs=placed,
        out_specs=P("replica", None, "fsdp"),
        check_vma=False,
    )
```

```python
from functools import partial

import jax
import jax.numpy as jnp
from jax import lax
from jax.experimental import pallas as pl
from jax.experimental.pallas import tpu as pltpu
from jax.sharding import PartitionSpec as P

HEAD = 128
ROWS = 256
STRIP = 32
PIECES = 4
PARTS = 4
MESH = pl.DeviceIdType.MESH


def kernel(
    peers,
    count,
    distance,
    features,
    cotangent,
    master,
    moment,
    variance,
    scalars,
    mixed,
    tokens,
    flipped,
    upstream,
    dquery,
    grads,
    params,
    first_in,
    second_in,
    outgoing,
    incoming,
    own_sem,
    go_sem,
    load_sem,
    feature_send,
    feature_recv,
    column_send,
    column_recv,
    gossip_send,
    gossip_recv,
):
    chunks, depth, _ = params.shape
    scale = depth ** (-0.5)
    replica, me = lax.axis_index("replica"), lax.axis_index("fsdp")
    target = lax.rem(replica + distance, count)
    source = lax.rem(replica + count - distance, count)
    odd = lax.rem(replica, 2)
    partner = replica + 1 - 2 * odd
    leads = odd == distance % 2

    def span(at, parts):
        size = depth // parts
        return pl.ds(pl.multiple_of(at * size, size), size)

    def columns(chunk):
        return pl.ds(pl.multiple_of(chunk * HEAD, HEAD), HEAD)

    def owned(chunk):
        return pltpu.make_async_copy(
            cotangent.at[0, :, columns(me * chunks + chunk)],
            upstream.at[chunk, 0],
            own_sem.at[1 + chunk],
        )

    def loads(chunk):
        return [
            pltpu.make_async_copy(
                whole.at[0, :, columns(chunk)], held.at[chunk], load_sem.at[at, chunk]
            )
            for at, (whole, held) in enumerate(
                ((master, params), (moment, first_in), (variance, second_in))
            )
        ]

    def features_to(step, piece):
        return pltpu.make_async_remote_copy(
            src_ref=features.at[0, :, span(piece, PIECES)],
            dst_ref=tokens.at[step, :, span(piece, PIECES)],
            send_sem=feature_send.at[step, piece],
            recv_sem=feature_recv.at[step, piece],
            device_id={"fsdp": lax.rem(me + step, peers)},
            device_id_type=MESH,
        )

    def columns_to(step, chunk):
        peer = lax.rem(me + step, peers)
        return pltpu.make_async_remote_copy(
            src_ref=cotangent.at[0, :, columns(peer * chunks + chunk)],
            dst_ref=upstream.at[chunk, step],
            send_sem=column_send.at[step, chunk],
            recv_sem=column_recv.at[step, chunk],
            device_id={"fsdp": peer},
            device_id_type=MESH,
        )

    def gossip(chunk, part):
        return pltpu.make_async_remote_copy(
            src_ref=outgoing.at[chunk, span(part, PARTS)],
            dst_ref=incoming.at[chunk, span(part, PARTS)],
            send_sem=gossip_send.at[chunk, part],
            recv_sem=gossip_recv.at[chunk, part],
            device_id={"replica": target},
            device_id_type=MESH,
        )

    def send_features():
        @pl.loop(1, peers)
        def _(step):
            for piece in range(PIECES):
                features_to(step, piece).start()
            columns_to(step, 0).start()

    def features_left(pieces):
        @pl.loop(1, peers)
        def _(step):
            for piece in pieces:
                features_to(step, piece).wait_send()

    barrier = pltpu.get_barrier_semaphore()
    for step in range(1, peers):
        pl.semaphore_signal(
            barrier, inc=1, device_id={"fsdp": lax.rem(me + step, peers)}, device_id_type=MESH
        )
    pl.semaphore_signal(barrier, inc=1, device_id={"replica": source}, device_id_type=MESH)
    pl.semaphore_signal(barrier, inc=1, device_id={"replica": partner}, device_id_type=MESH)
    own_features = pltpu.make_async_copy(features.at[0], tokens.at[0], own_sem.at[0])
    own_features.start()

    def load(chunk):
        owned(chunk).start()
        for copy in loads(chunk):
            copy.start()

    load(0)
    pl.semaphore_wait(barrier, peers + 1)

    @pl.when(leads)
    def _():
        send_features()

    pl.loop(1, chunks)(load)

    def flip(step, piece):
        blocks = depth // PIECES // ROWS

        @pl.loop(0, blocks)
        def _(block):
            at = (piece * blocks + block) * ROWS
            rows = pl.ds(pl.multiple_of(at, ROWS), ROWS)
            flipped[step, rows, :] = tokens[step, :, rows].T

    def arrived(chunk):
        owned(chunk).wait()
        for copy in loads(chunk):
            copy.wait()

    def weights_of(chunk):
        return params[chunk].astype(jnp.bfloat16)

    def backward(chunk, step, weights):
        query = jnp.dot(tokens[step], weights, preferred_element_type=jnp.float32) * scale
        inverse = lax.rsqrt(jnp.mean(query * query, axis=-1, keepdims=True) + 1e-06)
        normed = query * inverse
        cot = upstream[chunk, step].astype(jnp.float32)
        projected = jnp.mean(cot * normed, axis=-1, keepdims=True)
        dquery[step] = (inverse * (cot - normed * projected)).astype(jnp.bfloat16)

    own_features.wait()
    for piece in range(PIECES):
        flip(0, piece)
    arrived(0)
    backward(0, 0, weights_of(0))

    @pl.when(leads)
    def _():
        features_left(range(PIECES - 1))
        pl.semaphore_signal(go_sem, inc=1, device_id={"replica": partner}, device_id_type=MESH)

    @pl.when(jnp.logical_not(leads))
    def _():
        pl.semaphore_wait(go_sem, 1)
        send_features()

    @pl.loop(1, peers)
    def _(step):
        for piece in range(PIECES):
            features_to(step, piece).wait_recv()
            flip(step, piece)

    def send_columns(chunk):
        @pl.loop(1, peers)
        def _(step):
            columns_to(step, chunk).start()

    for chunk in range(1, min(3, chunks)):
        send_columns(chunk)

    of_variance, of_square, of_moment, of_grad = [scalars[at] for at in range(4)]

    def received(chunk, weights):
        @pl.loop(1, peers)
        def _(step):
            columns_to(step, chunk).wait_recv()
            backward(chunk, step, weights)

    def update(chunk):
        def revise(block):
            rows = pl.ds(pl.multiple_of(block * ROWS, ROWS), ROWS)
            total = jnp.dot(flipped[0, rows, :], dquery[0], preferred_element_type=jnp.float32)
            for step in range(1, peers):
                total += jnp.dot(
                    flipped[step, rows, :], dquery[step], preferred_element_type=jnp.float32
                )
            grads[...] = total
            for strip in range(ROWS // STRIP):
                rows = pl.ds(pl.multiple_of(block * ROWS + strip * STRIP, STRIP), STRIP)
                grad = grads[pl.ds(strip * STRIP, STRIP), :]
                moment_here = first_in[chunk, rows, :].astype(jnp.float32)
                square = of_variance * second_in[chunk, rows, :] + of_square * (grad * grad)
                root = lax.rsqrt(square)
                bottom = square * root + 1e-08
                inverse = root * (2.0 - bottom * root)
                top = of_moment * moment_here + of_grad * grad
                half = 0.495 * params[chunk, rows, :] - top * inverse
                params[chunk, rows, :] = half
                outgoing[chunk, rows, :] = half.astype(jnp.bfloat16)

        @pl.loop(0, PARTS)
        def _(part):
            blocks = depth // PARTS // ROWS

            @pl.loop(0, blocks)
            def _(block):
                revise(part * blocks + block)

            gossip(chunk, part).start()

    @pl.loop(0, chunks)
    def _(chunk):
        @pl.when(chunk > 0)
        def _():
            arrived(chunk)
            backward(chunk, 0, weights_of(chunk))

        @pl.when(chunk + 3 < chunks)
        def _():
            send_columns(chunk + 3)

        received(chunk, weights_of(chunk))
        update(chunk)

    @pl.loop(0, chunks)
    def _(chunk):
        @pl.loop(0, PARTS)
        def _(part):
            gossip(chunk, part).wait_recv()
            rows = span(part, PARTS)
            mixed[0, rows, columns(chunk)] = params[chunk, rows, :] + incoming[
                chunk, rows, :
            ].astype(jnp.float32)

    features_left([PIECES - 1])

    @pl.when(jnp.logical_not(leads))
    def _():
        features_left(range(PIECES - 1))

    @pl.loop(0, chunks)
    def _(chunk):
        for step in range(1, peers):
            columns_to(step, chunk).wait_send()
        for part in range(PARTS):
            gossip(chunk, part).wait_send()


def updated(features, cotangent, master, moment, variance, scalars, peers, count, distance, which):
    _, here, depth = features.shape
    local = master.shape[2]
    chunks = local // HEAD
    dma = pltpu.SemaphoreType.DMA
    values = depth * local
    return pl.pallas_call(
        partial(kernel, peers, count, distance),
        out_shape=pltpu.VMEM(master.shape, jnp.float32),
        in_specs=[pl.BlockSpec(memory_space=pl.ANY)] * 5
        + [pl.BlockSpec(memory_space=pltpu.SMEM)],
        out_specs=pl.BlockSpec(memory_space=pltpu.VMEM),
        scratch_shapes=[
            pltpu.VMEM((peers, here, depth), jnp.bfloat16),
            pltpu.VMEM((peers, depth, here), jnp.bfloat16),
            pltpu.VMEM((chunks, peers, here, HEAD), jnp.bfloat16),
            pltpu.VMEM((peers, here, HEAD), jnp.bfloat16),
            pltpu.VMEM((ROWS, HEAD), jnp.float32),
            pltpu.VMEM((chunks, depth, HEAD), jnp.float32),
            pltpu.VMEM((chunks, depth, HEAD), jnp.bfloat16),
            pltpu.VMEM((chunks, depth, HEAD), jnp.float32),
            pltpu.VMEM((chunks, depth, HEAD), jnp.bfloat16),
            pltpu.VMEM((chunks, depth, HEAD), jnp.bfloat16),
            dma((1 + chunks,)),
            pltpu.SemaphoreType.REGULAR,
            dma((3, chunks)),
            dma((peers, PIECES)),
            dma((peers, PIECES)),
            dma((peers, chunks)),
            dma((peers, chunks)),
            dma((chunks, PARTS)),
            dma((chunks, PARTS)),
        ],
        compiler_params=pltpu.CompilerParams(
            collective_id=which, has_side_effects=True, vmem_limit_bytes=52 * 1024 * 1024
        ),
        cost_estimate=pl.CostEstimate(
            flops=4 * peers * here * values, bytes_accessed=18 * values, transcendentals=values
        ),
        name=f"step_{distance}",
    )(features, cotangent, master, moment, variance, scalars)


def body(peers, count, features, cotangent, master, moment, variance, step_count):
    counter = step_count[0]
    power = counter.astype(jnp.float32)
    correct_first = 1.0 - jnp.power(jnp.float32(0.9), power)
    correct_second = 1.0 - jnp.power(jnp.float32(0.999), power)
    scale = master.shape[1] ** (-0.5)
    scalars = jnp.stack(
        [
            0.999 / correct_second,
            0.001 * scale * scale / correct_second,
            0.05 * 0.9 / correct_first,
            0.05 * 0.1 * scale / correct_first,
        ]
    )
    return lax.switch(
        counter % 4,
        [
            partial(updated, peers=peers, count=count, distance=1 << level, which=level)
            for level in range(4)
        ],
        features,
        cotangent,
        master,
        moment,
        variance,
        scalars,
    )


def solution(mesh):
    placed = (
        P("replica", "fsdp", None),
        P("replica", "fsdp", None),
        P("replica", None, "fsdp"),
        P("replica", None, "fsdp"),
        P("replica", None, "fsdp"),
        P(),
    )
    return jax.shard_map(
        partial(body, mesh.shape["fsdp"], mesh.shape["replica"]),
        mesh=mesh,
        in_specs=placed,
        out_specs=P("replica", None, "fsdp"),
        check_vma=False,
    )
```

```python
from functools import partial

import jax
import jax.numpy as jnp
from jax import lax
from jax.experimental import pallas as pl
from jax.experimental.pallas import tpu as pltpu
from jax.sharding import PartitionSpec as P

HEAD = 128
ROWS = 256
STRIP = 32
PIECES = 8
PARTS = 4
MESH = pl.DeviceIdType.MESH


def kernel(
    peers,
    count,
    distance,
    features,
    cotangent,
    master,
    moment,
    variance,
    scalars,
    mixed,
    tokens,
    flipped,
    upstream,
    dquery,
    grads,
    queries,
    params,
    first_in,
    second_in,
    outgoing,
    incoming,
    own_sem,
    go_sem,
    load_sem,
    feature_send,
    feature_recv,
    column_send,
    column_recv,
    gossip_send,
    gossip_recv,
):
    chunks, depth, _ = params.shape
    scale = depth ** (-0.5)
    replica, me = lax.axis_index("replica"), lax.axis_index("fsdp")
    target = lax.rem(replica + distance, count)
    source = lax.rem(replica + count - distance, count)
    odd = lax.rem(replica, 2)
    partner = replica + 1 - 2 * odd
    leads = odd == distance % 2

    def span(at, parts):
        size = depth // parts
        return pl.ds(pl.multiple_of(at * size, size), size)

    def columns(chunk):
        return pl.ds(pl.multiple_of(chunk * HEAD, HEAD), HEAD)

    def owned(chunk):
        return pltpu.make_async_copy(
            cotangent.at[0, :, columns(me * chunks + chunk)],
            upstream.at[chunk, 0],
            own_sem.at[1 + chunk],
        )

    def loads(chunk):
        return [
            pltpu.make_async_copy(
                whole.at[0, :, columns(chunk)], held.at[chunk], load_sem.at[at, chunk]
            )
            for at, (whole, held) in enumerate(
                ((master, params), (moment, first_in), (variance, second_in))
            )
        ]

    def features_to(step, piece):
        return pltpu.make_async_remote_copy(
            src_ref=features.at[0, :, span(piece, PIECES)],
            dst_ref=tokens.at[step, :, span(piece, PIECES)],
            send_sem=feature_send.at[step, piece],
            recv_sem=feature_recv.at[step, piece],
            device_id={"fsdp": lax.rem(me + step, peers)},
            device_id_type=MESH,
        )

    def columns_to(step, chunk):
        peer = lax.rem(me + step, peers)
        return pltpu.make_async_remote_copy(
            src_ref=cotangent.at[0, :, columns(peer * chunks + chunk)],
            dst_ref=upstream.at[chunk, step],
            send_sem=column_send.at[step, chunk],
            recv_sem=column_recv.at[step, chunk],
            device_id={"fsdp": peer},
            device_id_type=MESH,
        )

    def gossip(chunk, part):
        return pltpu.make_async_remote_copy(
            src_ref=outgoing.at[chunk, span(part, PARTS)],
            dst_ref=incoming.at[chunk, span(part, PARTS)],
            send_sem=gossip_send.at[chunk, part],
            recv_sem=gossip_recv.at[chunk, part],
            device_id={"replica": target},
            device_id_type=MESH,
        )

    def send_features():
        @pl.loop(1, peers)
        def _(step):
            for piece in range(PIECES):
                features_to(step, piece).start()
            columns_to(step, 0).start()

    def features_left(pieces):
        @pl.loop(1, peers)
        def _(step):
            for piece in pieces:
                features_to(step, piece).wait_send()

    barrier = pltpu.get_barrier_semaphore()
    for step in range(1, peers):
        pl.semaphore_signal(
            barrier, inc=1, device_id={"fsdp": lax.rem(me + step, peers)}, device_id_type=MESH
        )
    pl.semaphore_signal(barrier, inc=1, device_id={"replica": source}, device_id_type=MESH)
    pl.semaphore_signal(barrier, inc=1, device_id={"replica": partner}, device_id_type=MESH)
    own_features = pltpu.make_async_copy(features.at[0], tokens.at[0], own_sem.at[0])
    own_features.start()

    def load(chunk):
        owned(chunk).start()
        for copy in loads(chunk):
            copy.start()

    load(0)
    pl.semaphore_wait(barrier, peers + 1)

    @pl.when(leads)
    def _():
        send_features()

    pl.loop(1, chunks)(load)

    def flip(step, piece):
        blocks = depth // PIECES // ROWS

        @pl.loop(0, blocks)
        def _(block):
            at = (piece * blocks + block) * ROWS
            rows = pl.ds(pl.multiple_of(at, ROWS), ROWS)
            flipped[step, rows, :] = tokens[step, :, rows].T

    def arrived(chunk):
        owned(chunk).wait()
        for copy in loads(chunk):
            copy.wait()

    def weights_of(chunk):
        return params[chunk].astype(jnp.bfloat16)

    def project(step, weights):
        queries[step] = jnp.dot(tokens[step], weights, preferred_element_type=jnp.float32)

    def backward(chunk, step):
        query = queries[step] * scale
        inverse = lax.rsqrt(jnp.mean(query * query, axis=-1, keepdims=True) + 1e-06)
        normed = query * inverse
        cot = upstream[chunk, step].astype(jnp.float32)
        projected = jnp.mean(cot * normed, axis=-1, keepdims=True)
        dquery[step] = (inverse * (cot - normed * projected)).astype(jnp.bfloat16)

    own_features.wait()
    for piece in range(PIECES):
        flip(0, piece)
    arrived(0)
    project(0, weights_of(0))
    backward(0, 0)

    @pl.when(leads)
    def _():
        features_left(range(PIECES - 1))
        pl.semaphore_signal(go_sem, inc=1, device_id={"replica": partner}, device_id_type=MESH)

    @pl.when(jnp.logical_not(leads))
    def _():
        pl.semaphore_wait(go_sem, 1)
        send_features()

    @pl.loop(1, peers)
    def _(step):
        for piece in range(PIECES):
            features_to(step, piece).wait_recv()
            flip(step, piece)
            part = jnp.dot(
                tokens[step, :, span(piece, PIECES)],
                params[0, span(piece, PIECES), :].astype(jnp.bfloat16),
                preferred_element_type=jnp.float32,
            )
            queries[step] = part if piece == 0 else queries[step] + part

    def send_columns(chunk):
        @pl.loop(1, peers)
        def _(step):
            columns_to(step, chunk).start()

    for chunk in range(1, min(3, chunks)):
        send_columns(chunk)

    of_variance, of_square, of_moment, of_grad = [scalars[at] for at in range(4)]

    def received(chunk):
        @pl.loop(1, peers)
        def _(step):
            columns_to(step, chunk).wait_recv()
            backward(chunk, step)

    def update(chunk):
        def revise(block):
            rows = pl.ds(pl.multiple_of(block * ROWS, ROWS), ROWS)
            total = jnp.dot(flipped[0, rows, :], dquery[0], preferred_element_type=jnp.float32)
            for step in range(1, peers):
                total += jnp.dot(
                    flipped[step, rows, :], dquery[step], preferred_element_type=jnp.float32
                )
            grads[...] = total
            for strip in range(ROWS // STRIP):
                rows = pl.ds(pl.multiple_of(block * ROWS + strip * STRIP, STRIP), STRIP)
                grad = grads[pl.ds(strip * STRIP, STRIP), :]
                moment_here = first_in[chunk, rows, :].astype(jnp.float32)
                square = of_variance * second_in[chunk, rows, :] + of_square * (grad * grad)
                root = lax.rsqrt(square)
                bottom = square * root + 1e-08
                inverse = root * (2.0 - bottom * root)
                top = of_moment * moment_here + of_grad * grad
                half = 0.495 * params[chunk, rows, :] - top * inverse
                params[chunk, rows, :] = half
                outgoing[chunk, rows, :] = half.astype(jnp.bfloat16)

        @pl.loop(0, PARTS)
        def _(part):
            blocks = depth // PARTS // ROWS

            @pl.loop(0, blocks)
            def _(block):
                revise(part * blocks + block)

            gossip(chunk, part).start()

    @pl.loop(0, chunks)
    def _(chunk):
        @pl.when(chunk > 0)
        def _():
            arrived(chunk)
            weights = weights_of(chunk)

            @pl.loop(0, peers)
            def _(step):
                project(step, weights)

            backward(chunk, 0)

        @pl.when(chunk + 3 < chunks)
        def _():
            send_columns(chunk + 3)

        received(chunk)
        update(chunk)

    @pl.loop(0, chunks)
    def _(chunk):
        @pl.loop(0, PARTS)
        def _(part):
            gossip(chunk, part).wait_recv()
            rows = span(part, PARTS)
            mixed[0, rows, columns(chunk)] = params[chunk, rows, :] + incoming[
                chunk, rows, :
            ].astype(jnp.float32)

    features_left([PIECES - 1])

    @pl.when(jnp.logical_not(leads))
    def _():
        features_left(range(PIECES - 1))

    @pl.loop(0, chunks)
    def _(chunk):
        for step in range(1, peers):
            columns_to(step, chunk).wait_send()
        for part in range(PARTS):
            gossip(chunk, part).wait_send()


def updated(features, cotangent, master, moment, variance, scalars, peers, count, distance, which):
    _, here, depth = features.shape
    local = master.shape[2]
    chunks = local // HEAD
    dma = pltpu.SemaphoreType.DMA
    values = depth * local
    return pl.pallas_call(
        partial(kernel, peers, count, distance),
        out_shape=pltpu.VMEM(master.shape, jnp.float32),
        in_specs=[pl.BlockSpec(memory_space=pl.ANY)] * 5
        + [pl.BlockSpec(memory_space=pltpu.SMEM)],
        out_specs=pl.BlockSpec(memory_space=pltpu.VMEM),
        scratch_shapes=[
            pltpu.VMEM((peers, here, depth), jnp.bfloat16),
            pltpu.VMEM((peers, depth, here), jnp.bfloat16),
            pltpu.VMEM((chunks, peers, here, HEAD), jnp.bfloat16),
            pltpu.VMEM((peers, here, HEAD), jnp.bfloat16),
            pltpu.VMEM((ROWS, HEAD), jnp.float32),
            pltpu.VMEM((peers, here, HEAD), jnp.float32),
            pltpu.VMEM((chunks, depth, HEAD), jnp.float32),
            pltpu.VMEM((chunks, depth, HEAD), jnp.bfloat16),
            pltpu.VMEM((chunks, depth, HEAD), jnp.float32),
            pltpu.VMEM((chunks, depth, HEAD), jnp.bfloat16),
            pltpu.VMEM((chunks, depth, HEAD), jnp.bfloat16),
            dma((1 + chunks,)),
            pltpu.SemaphoreType.REGULAR,
            dma((3, chunks)),
            dma((peers, PIECES)),
            dma((peers, PIECES)),
            dma((peers, chunks)),
            dma((peers, chunks)),
            dma((chunks, PARTS)),
            dma((chunks, PARTS)),
        ],
        compiler_params=pltpu.CompilerParams(
            collective_id=which, has_side_effects=True, vmem_limit_bytes=52 * 1024 * 1024
        ),
        cost_estimate=pl.CostEstimate(
            flops=4 * peers * here * values, bytes_accessed=18 * values, transcendentals=values
        ),
        name=f"step_{distance}",
    )(features, cotangent, master, moment, variance, scalars)


def body(peers, count, features, cotangent, master, moment, variance, step_count):
    counter = step_count[0]
    power = counter.astype(jnp.float32)
    correct_first = 1.0 - jnp.power(jnp.float32(0.9), power)
    correct_second = 1.0 - jnp.power(jnp.float32(0.999), power)
    scale = master.shape[1] ** (-0.5)
    scalars = jnp.stack(
        [
            0.999 / correct_second,
            0.001 * scale * scale / correct_second,
            0.05 * 0.9 / correct_first,
            0.05 * 0.1 * scale / correct_first,
        ]
    )
    return lax.switch(
        counter % 4,
        [
            partial(updated, peers=peers, count=count, distance=1 << level, which=level)
            for level in range(4)
        ],
        features,
        cotangent,
        master,
        moment,
        variance,
        scalars,
    )


def solution(mesh):
    placed = (
        P("replica", "fsdp", None),
        P("replica", "fsdp", None),
        P("replica", None, "fsdp"),
        P("replica", None, "fsdp"),
        P("replica", None, "fsdp"),
        P(),
    )
    return jax.shard_map(
        partial(body, mesh.shape["fsdp"], mesh.shape["replica"]),
        mesh=mesh,
        in_specs=placed,
        out_specs=P("replica", None, "fsdp"),
        check_vma=False,
    )
```
